32 devices in a mesh: fx: 8 (over z, x), fy: 4 (over y, core).
Axes of the slice: x: 2, y: 2, z: 4, core: 2. Of those that a mesh axis runs over, the one named last changes fastest.
Arguments:
- air_state: float32 [2, 58, 128, 2048], P(None, None, 'fy', 'fx'), may hold values from -6 to 6
- jacobian: float32 [128, 2048], P('fy', 'fx'), may hold values from 0.5 to 2
- viscosity: float32 [128, 2048], P('fy', 'fx'), may hold values from 0.5 to 2
- mixing: float32 [58, 58], replicated, may hold values from -0.75 to 0.75
- convect_dest: int32 [128, 8], P('fy', 'fx'), may hold values from -1 to 7, as said below
Outputs:
- next_state: float32 [2, 58, 128, 2048], P(None, None, 'fy', 'fx')
The draws below stay inside these ranges and needn't reach their ends.
Inputs may be any that keep to these rules, and one draw needn't show every extreme that they name: `convect_dest`: in each fy row of devices, 2 devices have all their blocks convective and the others none; every fx index of that row is named by exactly 8 blocks of the row, and at most 4 blocks of one device name the same index.
All inputs are finite; a program needn't handle non-finite values.
Results may differ from the reference program's by a relative error of at most 0.00089.
Values may be sent and summed in bfloat16 or wider, within the bound.
A program may use at most 64 MiB of HBM per device.

```python
import math
import jax
import jax.numpy as jnp
import numpy as np
from jax import lax

EX = 64
EY = 8
LEV = 58
SUBSTEPS = 24
NX = 2048
NY = 128
N_FX = 8
N_FY = 4


def draw_convect_dest(key, part):
    key = jax.random.fold_in(key, 11)
    heavy_count = N_FX // 4
    block_rows = 4 * EY
    slot_total = N_FX * EY

    def one_row(row_key):
        key_heavy, key_target, key_order = jax.random.split(row_key, 3)
        heavy_devs = jax.random.permutation(key_heavy, N_FX)[:heavy_count]
        target = jax.random.permutation(key_target, N_FX)
        orders = jax.vmap(lambda inner: jax.random.permutation(inner, block_rows))(jax.random.split(key_order, heavy_count))
        position = jnp.arange(slot_total)
        source = position % heavy_count
        within = position // heavy_count
        dest_dev = target[position // EY].astype(jnp.int32)
        blank = jnp.full((block_rows, N_FX), -1, jnp.int32)
        return blank.at[orders[source, within], heavy_devs[source]].set(dest_dev)
    grid = jax.vmap(one_row)(jax.random.split(key, N_FY))
    return grid.reshape(N_FY * block_rows, N_FX)


def steps_of(own_key, dims, pieces, least, largest):
    gain = 1.0
    for dim, blocks in pieces:
        heights = jax.random.uniform(jax.random.fold_in(jax.random.fold_in(own_key, 6), dim), (blocks,), jnp.float32, least / len(pieces), largest / len(pieces))
        gain = gain * jnp.repeat(jnp.exp(heights), dims[dim] // blocks).reshape((-1,) + (1,) * (len(dims) - 1 - dim))
    return gain


def centred(own_key, extent, width, most, pieces=(), held_as=jnp.bfloat16):
    result = width * jax.random.normal(own_key, extent, jnp.float32)
    if pieces:
        result = result * steps_of(own_key, extent, pieces, -0.22, 0.18)
    return jnp.clip(result, -most, most).astype(held_as)


def setup_inputs(seed: int = 0) -> dict:
    streams_of = jax.random.split(jax.random.key(seed), 6)
    return {
        "air_state": centred(streams_of[0], (2, LEV, NY, NX), 1.0, 6.0, ((2, 4), (3, 8)), jnp.float32),
        "jacobian": jnp.clip(jnp.exp(math.log(2.0) - 1.3862944 * jax.random.uniform(streams_of[1], (NY, NX), jnp.float32) ** steps_of(streams_of[1], (NY, NX), ((0, 4), (1, 8)), -0.2, 0.2)), 0.5, 2.0),
        "viscosity": jnp.clip(jnp.exp(math.log(2.0) - 1.3862944 * jax.random.uniform(streams_of[2], (NY, NX), jnp.float32) ** steps_of(streams_of[2], (NY, NX), ((0, 4), (1, 8)), -0.2, 0.2)), 0.5, 2.0),
        "mixing": centred(streams_of[3], (LEV, LEV), LEV ** -0.5, 0.75, (), jnp.float32),
        "convect_dest": draw_convect_dest(jax.random.fold_in(streams_of[5], 71), 0),
    }


def gll_tables():
    nodes = np.array([-1.0, -1.0 / np.sqrt(5.0), 1.0 / np.sqrt(5.0), 1.0])
    gll_weight = np.array([1.0 / 6.0, 5.0 / 6.0, 5.0 / 6.0, 1.0 / 6.0])
    deriv = np.zeros((4, 4))
    for first in range(4):
        for second in range(4):
            if first == second:
                deriv[first, second] = sum((1.0 / (nodes[first] - nodes[other]) for other in range(4) if other != first))
            else:
                top = np.prod([nodes[first] - nodes[other] for other in range(4) if other != first])
                below = np.prod([nodes[second] - nodes[other] for other in range(4) if other != second])
                deriv[first, second] = top / below / (nodes[first] - nodes[second])
    stiff = deriv.T * gll_weight[None, :] @ deriv
    return (stiff, gll_weight)

def summation(grid_vals):
    col_index = jnp.arange(grid_vals.shape[-1]) % 4
    row_index = (jnp.arange(grid_vals.shape[-2]) % 4)[:, None]
    along = grid_vals + jnp.where(col_index == 3, jnp.roll(grid_vals, -1, -1), jnp.where(col_index == 0, jnp.roll(grid_vals, 1, -1), 0.0))
    return along + jnp.where(row_index == 3, jnp.roll(along, -1, -2), jnp.where(row_index == 0, jnp.roll(along, 1, -2), 0.0))

def reference(air_state, jacobian, viscosity, mixing, convect_dest):
    high = lax.Precision.HIGHEST
    stiff, gll_weight = gll_tables()
    stiff_mat = jnp.asarray(stiff, jnp.float32)
    row_total, col_total = (air_state.shape[2], air_state.shape[3])
    weight_rows = jnp.asarray(np.tile(gll_weight, row_total // 4), jnp.float32)
    weight_cols = jnp.asarray(np.tile(gll_weight, col_total // 4), jnp.float32)
    along_term = jnp.einsum('ab,flyeb->flyea', stiff_mat, air_state.reshape(2, LEV, row_total, col_total // 4, 4), precision=high).reshape(air_state.shape)
    across_term = jnp.einsum('ab,flebx->fleax', stiff_mat, air_state.reshape(2, LEV, row_total // 4, 4, col_total), precision=high).reshape(air_state.shape)
    local_term = -viscosity * (weight_rows[:, None] * along_term + weight_cols[None, :] * across_term)
    mass = jacobian * (weight_rows[:, None] * weight_cols[None, :])
    stacked = jnp.concatenate([local_term.reshape(2 * LEV, row_total, col_total), mass[None]], axis=0)
    summed = summation(stacked)
    dynamics = (summed[:-1] / summed[-1]).reshape(air_state.shape)
    snapshot = lax.optimization_barrier(air_state.astype(jnp.bfloat16)).astype(jnp.float32)

    def substep(index, carry):
        temper, moist = carry
        cond = jax.nn.softplus(moist - 0.5 * temper)
        temper = temper + 0.25 * jnp.einsum('lm,myx->lyx', mixing, cond, precision=high)
        moist = moist - 0.25 * cond
        return (temper, moist)
    temper, moist = lax.fori_loop(0, SUBSTEPS, substep, (snapshot[0], snapshot[1]))
    physics = jnp.stack([temper - snapshot[0], moist - snapshot[1]])
    convective = jnp.repeat(convect_dest >= 0, 4 * EX, axis=1)
    return air_state + 0.05 * dynamics + jnp.where(convective, physics, 0.0)
```

```python
import jax
import jax.numpy as jnp
import numpy as np
from jax import lax
from jax.experimental import pallas as pl
from jax.experimental.pallas import tpu as pltpu
from jax.sharding import PartitionSpec as P

SUBSTEPS = 24
LOG2E = float(np.log2(np.e))
LN2 = float(np.log(2.0))
LANES = 128
TILE = 8
F32 = jnp.float32
BF16 = jnp.bfloat16


def gll_tables():
    nodes = np.array([-1.0, -1.0 / np.sqrt(5.0), 1.0 / np.sqrt(5.0), 1.0])
    gll_weight = np.array([1.0 / 6.0, 5.0 / 6.0, 5.0 / 6.0, 1.0 / 6.0])
    deriv = np.zeros((4, 4))
    for first in range(4):
        for second in range(4):
            if first == second:
                deriv[first, second] = sum(
                    (1.0 / (nodes[first] - nodes[other]) for other in range(4) if other != first)
                )
            else:
                top = np.prod([nodes[first] - nodes[other] for other in range(4) if other != first])
                below = np.prod(
                    [nodes[second] - nodes[other] for other in range(4) if other != second]
                )
                deriv[first, second] = top / below / (nodes[first] - nodes[second])
    stiff = deriv.T * gll_weight[None, :] @ deriv
    return (stiff, gll_weight)


def by_node(index, values):
    node = index % 4
    result = jnp.full(index.shape, values[0], F32)
    for k in range(1, 4):
        result = jnp.where(node == k, F32(values[k]), result)
    return result


def split(value):
    high = value.astype(BF16)
    low = (value - high.astype(F32)).astype(BF16)
    return high, low


def sum_cols(g):
    n = g.shape[-1]
    col = lax.broadcasted_iota(jnp.int32, g.shape, 1)
    upper = pltpu.roll(g, n - 1, 1)
    lower = pltpu.roll(g, 1, 1)
    up = (col % 4 == 3) & (col != n - 1)
    low = (col % 4 == 0) & (col != 0)
    return g + jnp.where(up, upper, jnp.where(low, lower, 0.0))


def sum_rows(g, first=0.0, last=0.0):
    n = g.shape[0]
    row = lax.broadcasted_iota(jnp.int32, g.shape, 0)
    upper = jnp.where(row == n - 1, last, pltpu.roll(g, n - 1, 0))
    lower = jnp.where(row == 0, first, pltpu.roll(g, 1, 0))
    return g + jnp.where(row % 4 == 3, upper, jnp.where(row % 4 == 0, lower, 0.0))


def local_kernel(
    air, jac, visc, khi, klo, summed, msum, col_lo, col_hi, row_lo, row_hi, along, fa, fb
):
    step = pl.program_id(0)
    chunk, rows, cols = air.shape
    stiff, weight = gll_tables()

    @pl.when(step == 0)
    def _():
        r = lax.broadcasted_iota(jnp.int32, (rows, cols), 0)
        c = lax.broadcasted_iota(jnp.int32, (rows, cols), 1)
        wr, wc = by_node(r, weight), by_node(c, weight)
        fa[...] = -visc[...] * wr
        fb[...] = -visc[...] * wc
        mass = jac[...] * (wr * wc)
        msum[...] = sum_rows(sum_cols(mass))
        slot = pl.num_programs(0) * chunk
        lane = lax.broadcasted_iota(jnp.int32, (rows, LANES), 1)
        col_lo[...] = jnp.where(lane == slot, pltpu.roll(mass[:, :LANES], slot % LANES, 1), 0.0)
        col_hi[...] = jnp.where(
            lane == slot, pltpu.roll(mass[:, cols - LANES :], (slot + 1) % LANES, 1), 0.0
        )
        row_lo[...] = jnp.zeros_like(row_lo)
        row_hi[...] = jnp.zeros_like(row_hi)
        row_lo[pl.ds(slot, 1), :] = mass[0:1, :]
        row_hi[pl.ds(slot, 1), :] = mass[rows - 1 :, :]

    high, low = split(air[...].reshape(chunk * rows, cols))
    along[...] = (
        jnp.dot(high, khi[...], preferred_element_type=F32)
        + jnp.dot(low, khi[...], preferred_element_type=F32)
        + jnp.dot(high, klo[...], preferred_element_type=F32)
    ).reshape(chunk, rows, cols)

    sub = lax.broadcasted_iota(jnp.int32, (TILE, cols), 0)
    coefs = []
    for d in range(-3, 4):
        values = [stiff[k, k + d] if 0 <= k + d < 4 else 0.0 for k in range(4)]
        coefs.append((d, by_node(sub, values)))

    def level(i, _):
        index = step * chunk + i
        f = air[i].reshape(rows // TILE, TILE, cols)
        across = jnp.zeros_like(f)
        for d, coef in coefs:
            moved = f if d == 0 else pltpu.roll(f, (-d) % TILE, 1)
            across = across + coef[None] * moved
        local = fa[...] * along[i] + fb[...] * across.reshape(rows, cols)
        lane = lax.broadcasted_iota(jnp.int32, (rows, LANES), 1)
        mine = lane == index
        col_lo[...] = jnp.where(mine, pltpu.roll(local[:, :LANES], index, 1), col_lo[...])
        col_hi[...] = jnp.where(
            mine, pltpu.roll(local[:, cols - LANES :], index + 1, 1), col_hi[...]
        )
        row_lo[pl.ds(index, 1), :] = local[0:1, :]
        row_hi[pl.ds(index, 1), :] = local[rows - 1 :, :]
        summed[i] = sum_rows(sum_cols(local))
        return 0

    lax.fori_loop(0, chunk, level, 0, unroll=2 if chunk % 2 == 0 else 1)


def softplus2(y):
    return jnp.maximum(y, 0.0) + jnp.log2(1.0 + jnp.exp2(-jnp.abs(y)))


def physics_kernel(flag, mixing, air, out, y, csum):
    levels, rows, cols = air.shape[1:]
    depth = y.shape[1]

    @pl.when(flag[0] > 0)
    def _():
        t = air[0].astype(BF16).astype(F32)
        q = air[1].astype(BF16).astype(F32)
        x = (q - 0.5 * t) * LOG2E
        y[...] = jnp.zeros_like(y)
        csum[...] = jnp.zeros_like(csum)
        for r in range(rows):
            y[r, :levels, :] = x[:, r, :]
        eye = lax.broadcasted_iota(jnp.int32, (depth, depth), 0) == lax.broadcasted_iota(
            jnp.int32, (depth, depth), 1
        )
        mix = mixing[...]
        ahigh, alow = split(0.125 * mix + jnp.where(eye, 0.25, 0.0))
        acat = jnp.concatenate([ahigh, ahigh, alow], axis=1)

        def substep(_, carry):
            for r in range(rows):
                value = y[r]
                cond = softplus2(value)
                csum[r] += cond
                high, low = split(cond)
                stack = jnp.concatenate([high, low, high], axis=0)
                y[r] = value - jnp.dot(acat, stack, preferred_element_type=F32)
            return carry

        lax.fori_loop(0, SUBSTEPS, substep, 0)
        mhigh, mlow = split(0.25 * mix)
        mcat = jnp.concatenate([mhigh, mhigh, mlow], axis=1)
        for r in range(rows):
            total = csum[r] * LN2
            high, low = split(total)
            stack = jnp.concatenate([high, low, high], axis=0)
            heat = jnp.dot(mcat, stack, preferred_element_type=F32)
            out[0, :, r, :] = heat[:levels]
            out[1, :, r, :] = -0.25 * total[:levels]


def final_kernel(
    flag, air, summed, phys, msum, left, right, below, above, lb, la, rb, ra, out,
    inv, edge_l, edge_r, edge_b, edge_a,
):
    step = pl.program_id(0)
    chunk, rows, cols = air.shape
    row = lax.broadcasted_iota(jnp.int32, (rows, cols), 0)
    col = lax.broadcasted_iota(jnp.int32, (rows, cols), 1)

    def full(base, index):
        west = pltpu.roll(edge_l[...], (LANES - index) % LANES, 1)
        east = pltpu.roll(edge_r[...], (2 * LANES - 1 - index) % LANES, 1)
        zero = jnp.zeros((rows, cols - LANES), F32)
        base = base + jnp.where(col == 0, jnp.concatenate([west, zero], axis=1), 0.0)
        base = base + jnp.where(col == cols - 1, jnp.concatenate([zero, east], axis=1), 0.0)
        base = base + jnp.where(row == 0, edge_b[pl.ds(index, 1), :], 0.0)
        return base + jnp.where(row == rows - 1, edge_a[pl.ds(index, 1), :], 0.0)

    @pl.when(step == 0)
    def _():
        edge_l[...] = sum_rows(left[...], lb[...], la[...])
        edge_r[...] = sum_rows(right[...], rb[...], ra[...])
        edge_b[...] = sum_cols(below[...])
        edge_a[...] = sum_cols(above[...])
        inv[...] = 0.05 / full(msum[...], pl.num_programs(0) * chunk)

    def levels_with(extra):
        def level(i, _):
            total = full(summed[i], step * chunk + i)
            value = air[i] + inv[...] * total
            if extra:
                value = value + phys[i]
            out[i] = value
            return 0

        lax.fori_loop(0, chunk, level, 0)

    @pl.when(flag[0] > 0)
    def _():
        levels_with(True)

    @pl.when(flag[0] <= 0)
    def _():
        levels_with(False)


def body(air_state, jacobian, viscosity, mixing, convect_dest):
    _, levels, rows, cols = air_state.shape
    planes = 2 * levels
    chunk = levels // 2
    steps = planes // chunk
    flat = air_state.reshape(planes, rows, cols)
    stiff, _ = gll_tables()
    along_mat = np.kron(np.eye(cols // 4), stiff).astype(np.float32)
    khi = along_mat.astype(jnp.bfloat16)
    klo = (along_mat - khi.astype(np.float32)).astype(jnp.bfloat16)
    row_slots = -(-(planes + 1) // TILE) * TILE
    flag = (convect_dest[:1, 0] >= 0).astype(jnp.int32)

    def whole(shape):
        return pl.BlockSpec(shape, lambda *_: (0,) * len(shape))

    plane_spec = pl.BlockSpec((chunk, rows, cols), lambda i, *_: (i, 0, 0))
    plane = jax.ShapeDtypeStruct((planes, rows, cols), F32)
    edge_col = jax.ShapeDtypeStruct((rows, LANES), F32)
    edge_row = jax.ShapeDtypeStruct((row_slots, cols), F32)
    summed, msum, col_lo, col_hi, row_lo, row_hi = pl.pallas_call(
        local_kernel,
        grid=(steps,),
        out_shape=[
            plane, jax.ShapeDtypeStruct((rows, cols), F32), edge_col, edge_col, edge_row, edge_row,
        ],
        in_specs=[plane_spec] + [whole((rows, cols))] * 2 + [whole((cols, cols))] * 2,
        out_specs=[
            plane_spec, whole((rows, cols)), whole((rows, LANES)), whole((rows, LANES)),
            whole((row_slots, cols)), whole((row_slots, cols)),
        ],
        scratch_shapes=[
            pltpu.VMEM((chunk, rows, cols), F32),
            pltpu.VMEM((rows, cols), F32),
            pltpu.VMEM((rows, cols), F32),
        ],
        compiler_params=pltpu.CompilerParams(vmem_limit_bytes=32 * 2**20),
        name="local_terms",
    )(flat, jacobian, viscosity, khi, klo)

    nx, ny = lax.axis_size("fx"), lax.axis_size("fy")

    def shifted(value, dx, dy):
        if dy == 0:
            pairs = [((i + dx) % nx, i) for i in range(nx)]
            return lax.ppermute(value, "fx", pairs)
        if dx == 0:
            pairs = [((j + dy) % ny, j) for j in range(ny)]
            return lax.ppermute(value, "fy", pairs)
        pairs = [
            (((i + dx) % nx) * ny + (j + dy) % ny, i * ny + j) for i in range(nx) for j in range(ny)
        ]
        return lax.ppermute(value, ("fx", "fy"), pairs)

    left, right = shifted(col_hi, -1, 0), shifted(col_lo, 1, 0)
    below, above = shifted(row_hi, 0, -1), shifted(row_lo, 0, 1)
    lb, la = shifted(col_hi[rows - 1 :], -1, -1), shifted(col_hi[:1], -1, 1)
    rb, ra = shifted(col_lo[rows - 1 :], 1, -1), shifted(col_lo[:1], 1, 1)

    depth = -(-levels // 16) * 16
    mix = jnp.zeros((depth, depth), F32).at[:levels, :levels].set(mixing)
    group = TILE
    air_spec = pl.BlockSpec(
        (2, levels, group, cols), lambda i, flag: (0, 0, i * flag[0], 0)
    )
    phys = pl.pallas_call(
        physics_kernel,
        grid_spec=pltpu.PrefetchScalarGridSpec(
            num_scalar_prefetch=1,
            grid=(rows // group,),
            in_specs=[whole((depth, depth)), air_spec],
            out_specs=air_spec,
            scratch_shapes=[pltpu.VMEM((group, depth, cols), F32)] * 2,
        ),
        out_shape=jax.ShapeDtypeStruct(air_state.shape, F32),
        compiler_params=pltpu.CompilerParams(vmem_limit_bytes=32 * 2**20),
        cost_estimate=pl.CostEstimate(
            flops=2 * SUBSTEPS * rows * cols * depth * depth * 6,
            bytes_accessed=16 * levels * rows * cols,
            transcendentals=2 * SUBSTEPS * rows * cols * depth,
        ),
        name="column_physics",
    )(flag, mix, air_state)

    phys_spec = pl.BlockSpec((chunk, rows, cols), lambda i, flag: (i * flag[0], 0, 0))
    result = pl.pallas_call(
        final_kernel,
        grid_spec=pltpu.PrefetchScalarGridSpec(
            num_scalar_prefetch=1,
            grid=(steps,),
            in_specs=[
                plane_spec, plane_spec, phys_spec, whole((rows, cols)),
                whole((rows, LANES)), whole((rows, LANES)),
                whole((row_slots, cols)), whole((row_slots, cols)),
            ] + [whole((1, LANES))] * 4,
            out_specs=plane_spec,
            scratch_shapes=[
                pltpu.VMEM((rows, cols), F32),
                pltpu.VMEM((rows, LANES), F32),
                pltpu.VMEM((rows, LANES), F32),
                pltpu.VMEM((row_slots, cols), F32),
                pltpu.VMEM((row_slots, cols), F32),
            ],
        ),
        out_shape=plane,
        compiler_params=pltpu.CompilerParams(vmem_limit_bytes=32 * 2**20),
        name="step_sum",
    )(flag, flat, summed, phys.reshape(planes, rows, cols), msum, left, right, below, above,
      lb, la, rb, ra)
    return result.reshape(air_state.shape)


def solution(mesh):
    placed = (P(None, None, "fy", "fx"), P("fy", "fx"), P("fy", "fx"), P(), P("fy", "fx"))
    return jax.shard_map(
        body, mesh=mesh, in_specs=placed, out_specs=P(None, None, "fy", "fx"), check_vma=False
    )
```

```python
import functools

import jax
import jax.numpy as jnp
import numpy as np
from jax import lax
from jax.experimental import pallas as pl
from jax.experimental.pallas import tpu as pltpu
from jax.sharding import PartitionSpec as P

SUBSTEPS = 24
LOG2E = float(np.log2(np.e))
LN2 = float(np.log(2.0))
LANES = 128
TILE = 8
F32 = jnp.float32
BF16 = jnp.bfloat16


def gll_tables():
    nodes = np.array([-1.0, -1.0 / np.sqrt(5.0), 1.0 / np.sqrt(5.0), 1.0])
    gll_weight = np.array([1.0 / 6.0, 5.0 / 6.0, 5.0 / 6.0, 1.0 / 6.0])
    deriv = np.zeros((4, 4))
    for first in range(4):
        for second in range(4):
            if first == second:
                deriv[first, second] = sum(
                    (1.0 / (nodes[first] - nodes[other]) for other in range(4) if other != first)
                )
            else:
                top = np.prod([nodes[first] - nodes[other] for other in range(4) if other != first])
                below = np.prod(
                    [nodes[second] - nodes[other] for other in range(4) if other != second]
                )
                deriv[first, second] = top / below / (nodes[first] - nodes[second])
    stiff = deriv.T * gll_weight[None, :] @ deriv
    return (stiff, gll_weight)


def by_node(index, values):
    node = index % 4
    result = jnp.full(index.shape, values[0], F32)
    for k in range(1, 4):
        result = jnp.where(node == k, F32(values[k]), result)
    return result


def split(value):
    high = value.astype(BF16)
    low = (value - high.astype(F32)).astype(BF16)
    return high, low


def repeat(count, width, work):
    def several(k, _):
        for u in range(width):
            work(k * width + u)
        return 0

    lax.fori_loop(0, count // width, several, 0)
    for i in range(count // width * width, count):
        work(i)


def sum_cols(g):
    n = g.shape[-1]
    col = lax.broadcasted_iota(jnp.int32, g.shape, 1)
    upper = pltpu.roll(g, n - 1, 1)
    lower = pltpu.roll(g, 1, 1)
    up = (col % 4 == 3) & (col != n - 1)
    low = (col % 4 == 0) & (col != 0)
    return g + jnp.where(up, upper, jnp.where(low, lower, 0.0))


def sum_rows(g, first=0.0, last=0.0):
    n = g.shape[0]
    row = lax.broadcasted_iota(jnp.int32, g.shape, 0)
    upper = jnp.where(row == n - 1, last, pltpu.roll(g, n - 1, 0))
    lower = jnp.where(row == 0, first, pltpu.roll(g, 1, 0))
    return g + jnp.where(row % 4 == 3, upper, jnp.where(row % 4 == 0, lower, 0.0))


def local_kernel(
    air, jac, visc, khi, klo, summed, msum, col_lo, col_hi, row_lo, row_hi, along, fa, fb
):
    step = pl.program_id(0)
    chunk, rows, cols = air.shape
    stiff, weight = gll_tables()

    @pl.when(step == 0)
    def _():
        r = lax.broadcasted_iota(jnp.int32, (rows, cols), 0)
        c = lax.broadcasted_iota(jnp.int32, (rows, cols), 1)
        wr, wc = by_node(r, weight), by_node(c, weight)
        fa[...] = -visc[...] * wr
        fb[...] = -visc[...] * wc
        mass = jac[...] * (wr * wc)
        msum[...] = sum_rows(sum_cols(mass))
        slot = pl.num_programs(0) * chunk
        lane = lax.broadcasted_iota(jnp.int32, (rows, LANES), 1)
        col_lo[...] = jnp.where(lane == slot, pltpu.roll(mass[:, :LANES], slot % LANES, 1), 0.0)
        col_hi[...] = jnp.where(
            lane == slot, pltpu.roll(mass[:, cols - LANES :], (slot + 1) % LANES, 1), 0.0
        )
        row_lo[...] = jnp.zeros_like(row_lo)
        row_hi[...] = jnp.zeros_like(row_hi)
        row_lo[pl.ds(slot, 1), :] = mass[0:1, :]
        row_hi[pl.ds(slot, 1), :] = mass[rows - 1 :, :]

    high, low = split(air[...].reshape(chunk * rows, cols))
    along[...] = (
        jnp.dot(high, khi[...], preferred_element_type=F32)
        + jnp.dot(low, khi[...], preferred_element_type=F32)
        + jnp.dot(high, klo[...], preferred_element_type=F32)
    ).reshape(chunk, rows, cols)

    sub = lax.broadcasted_iota(jnp.int32, (TILE, cols), 0)
    coefs = []
    for d in range(-3, 4):
        values = [stiff[k, k + d] if 0 <= k + d < 4 else 0.0 for k in range(4)]
        coefs.append((d, by_node(sub, values)))

    def level(i):
        index = step * chunk + i
        f = air[i].reshape(rows // TILE, TILE, cols)
        across = jnp.zeros_like(f)
        for d, coef in coefs:
            moved = f if d == 0 else pltpu.roll(f, (-d) % TILE, 1)
            across = across + coef[None] * moved
        local = fa[...] * along[i] + fb[...] * across.reshape(rows, cols)
        lane = lax.broadcasted_iota(jnp.int32, (rows, LANES), 1)
        mine = lane == index
        col_lo[...] = jnp.where(mine, pltpu.roll(local[:, :LANES], index, 1), col_lo[...])
        col_hi[...] = jnp.where(
            mine, pltpu.roll(local[:, cols - LANES :], index + 1, 1), col_hi[...]
        )
        row_lo[pl.ds(index, 1), :] = local[0:1, :]
        row_hi[pl.ds(index, 1), :] = local[rows - 1 :, :]
        summed[i] = sum_rows(sum_cols(local))

    repeat(chunk, 4, level)


def softplus2(y):
    return jnp.maximum(y, jnp.log2(1.0 + jnp.exp2(jnp.minimum(y, 100.0))))


def physics_kernel(flag, mixing, air, out, y, csum):
    levels, rows, cols = air.shape[1:]
    depth = y.shape[1]

    @pl.when(flag[0] > 0)
    def _():
        t = air[0].astype(BF16).astype(F32)
        q = air[1].astype(BF16).astype(F32)
        x = (q - 0.5 * t) * LOG2E
        y[...] = jnp.zeros_like(y)
        csum[...] = jnp.zeros_like(csum)
        for r in range(rows):
            y[r, :levels, :] = x[:, r, :]
        eye = lax.broadcasted_iota(jnp.int32, (depth, depth), 0) == lax.broadcasted_iota(
            jnp.int32, (depth, depth), 1
        )
        mix = mixing[...]
        ahigh, alow = split(0.125 * mix + jnp.where(eye, 0.25, 0.0))
        acat = jnp.concatenate([ahigh, ahigh, alow], axis=1)

        def substep(_, carry):
            for r in range(rows):
                value = y[r]
                cond = softplus2(value)
                csum[r] += cond
                high, low = split(cond)
                stack = jnp.concatenate([high, low, high], axis=0)
                y[r] = value - jnp.dot(acat, stack, preferred_element_type=F32)
            return carry

        lax.fori_loop(0, SUBSTEPS, substep, 0, unroll=4)
        mhigh, mlow = split(0.25 * mix)
        mcat = jnp.concatenate([mhigh, mhigh, mlow], axis=1)
        for r in range(rows):
            total = csum[r] * LN2
            high, low = split(total)
            stack = jnp.concatenate([high, low, high], axis=0)
            heat = jnp.dot(mcat, stack, preferred_element_type=F32)
            out[0, :, r, :] = heat[:levels]
            out[1, :, r, :] = -0.25 * total[:levels]


def edge_kernel(
    nx, ny, col_lo, col_hi, row_lo, row_hi, edge_l, edge_r, edge_b, edge_a,
    cols_in, rows_in, corners_in, send, recv,
):
    rows = col_lo.shape[0]
    x, y = lax.axis_index("fx"), lax.axis_index("fy")
    west, east = lax.rem(x + nx - 1, nx), lax.rem(x + 1, nx)
    south, north = lax.rem(y + ny - 1, ny), lax.rem(y + 1, ny)
    around = [
        (west, y), (east, y), (x, south), (x, north),
        (west, south), (west, north), (east, south), (east, north),
    ]
    barrier = pltpu.get_barrier_semaphore()
    for device in around:
        pl.semaphore_signal(
            barrier, inc=1, device_id=device, device_id_type=pl.DeviceIdType.MESH
        )
    pl.semaphore_wait(barrier, len(around))
    first, last = pl.ds(0, TILE), pl.ds(rows - TILE, TILE)
    moves = [
        (row_hi, rows_in.at[0], around[3]),
        (row_lo, rows_in.at[1], around[2]),
        (col_hi, cols_in.at[0], around[1]),
        (col_lo, cols_in.at[1], around[0]),
        (col_hi.at[last], corners_in.at[0], around[7]),
        (col_hi.at[first], corners_in.at[1], around[6]),
        (col_lo.at[last], corners_in.at[2], around[5]),
        (col_lo.at[first], corners_in.at[3], around[4]),
    ]
    copies = []
    for k, (source, target, device) in enumerate(moves):
        copy = pltpu.make_async_remote_copy(
            src_ref=source, dst_ref=target, send_sem=send.at[k], recv_sem=recv.at[k],
            device_id=device, device_id_type=pl.DeviceIdType.MESH,
        )
        copy.start()
        copies.append(copy)
    for copy in copies:
        copy.wait()
    edge_l[...] = sum_rows(cols_in[0], corners_in[0, TILE - 1 :, :], corners_in[1, :1, :])
    edge_r[...] = sum_rows(cols_in[1], corners_in[2, TILE - 1 :, :], corners_in[3, :1, :])
    edge_b[...] = sum_cols(rows_in[0])
    edge_a[...] = sum_cols(rows_in[1])


def final_kernel(
    flag, air, summed, phys, msum, edge_l, edge_r, edge_b, edge_a, out, inv
):
    step = pl.program_id(0)
    chunk, rows, cols = air.shape
    row = lax.broadcasted_iota(jnp.int32, (rows, cols), 0)
    col = lax.broadcasted_iota(jnp.int32, (rows, cols), 1)

    def full(base, index):
        west = pltpu.roll(edge_l[...], (LANES - index) % LANES, 1)
        east = pltpu.roll(edge_r[...], (2 * LANES - 1 - index) % LANES, 1)
        zero = jnp.zeros((rows, cols - LANES), F32)
        base = base + jnp.where(col == 0, jnp.concatenate([west, zero], axis=1), 0.0)
        base = base + jnp.where(col == cols - 1, jnp.concatenate([zero, east], axis=1), 0.0)
        base = base + jnp.where(row == 0, edge_b[pl.ds(index, 1), :], 0.0)
        return base + jnp.where(row == rows - 1, edge_a[pl.ds(index, 1), :], 0.0)

    @pl.when(step == 0)
    def _():
        inv[...] = 0.05 / full(msum[...], pl.num_programs(0) * chunk)

    def levels_with(extra):
        def level(i):
            total = full(summed[i], step * chunk + i)
            value = air[i] + inv[...] * total
            if extra:
                value = value + phys[i]
            out[i] = value

        repeat(chunk, 4, level)

    @pl.when(flag[0] > 0)
    def _():
        levels_with(True)

    @pl.when(flag[0] <= 0)
    def _():
        levels_with(False)


def body(air_state, jacobian, viscosity, mixing, convect_dest):
    _, levels, rows, cols = air_state.shape
    planes = 2 * levels
    chunk = levels // 2
    steps = planes // chunk
    flat = air_state.reshape(planes, rows, cols)
    stiff, _ = gll_tables()
    along_mat = np.kron(np.eye(cols // 4), stiff).astype(np.float32)
    khi = along_mat.astype(jnp.bfloat16)
    klo = (along_mat - khi.astype(np.float32)).astype(jnp.bfloat16)
    row_slots = -(-(planes + 1) // TILE) * TILE
    flag = (convect_dest[:1, 0] >= 0).astype(jnp.int32)

    def whole(shape):
        return pl.BlockSpec(shape, lambda *_: (0,) * len(shape))

    plane_spec = pl.BlockSpec((chunk, rows, cols), lambda i, *_: (i, 0, 0))
    plane = jax.ShapeDtypeStruct((planes, rows, cols), F32)
    edge_col = jax.ShapeDtypeStruct((rows, LANES), F32)
    edge_row = jax.ShapeDtypeStruct((row_slots, cols), F32)
    summed, msum, col_lo, col_hi, row_lo, row_hi = pl.pallas_call(
        local_kernel,
        grid=(steps,),
        out_shape=[
            plane, jax.ShapeDtypeStruct((rows, cols), F32), edge_col, edge_col, edge_row, edge_row,
        ],
        in_specs=[plane_spec] + [whole((rows, cols))] * 2 + [whole((cols, cols))] * 2,
        out_specs=[
            plane_spec, whole((rows, cols)), whole((rows, LANES)), whole((rows, LANES)),
            whole((row_slots, cols)), whole((row_slots, cols)),
        ],
        scratch_shapes=[
            pltpu.VMEM((chunk, rows, cols), F32),
            pltpu.VMEM((rows, cols), F32),
            pltpu.VMEM((rows, cols), F32),
        ],
        compiler_params=pltpu.CompilerParams(vmem_limit_bytes=32 * 2**20),
        name="local_terms",
    )(flat, jacobian, viscosity, khi, klo)

    nx, ny = lax.axis_size("fx"), lax.axis_size("fy")

    vmem = pl.BlockSpec(memory_space=pltpu.VMEM)
    edges = pl.pallas_call(
        functools.partial(edge_kernel, nx, ny),
        out_shape=[edge_col, edge_col, edge_row, edge_row],
        in_specs=[vmem] * 4,
        out_specs=[vmem] * 4,
        scratch_shapes=[
            pltpu.VMEM((2, rows, LANES), F32),
            pltpu.VMEM((2, row_slots, cols), F32),
            pltpu.VMEM((4, TILE, LANES), F32),
            pltpu.SemaphoreType.DMA((8,)),
            pltpu.SemaphoreType.DMA((8,)),
        ],
        compiler_params=pltpu.CompilerParams(collective_id=0, has_side_effects=True),
        name="edge_exchange",
    )(col_lo, col_hi, row_lo, row_hi)

    depth = -(-levels // 16) * 16
    mix = jnp.zeros((depth, depth), F32).at[:levels, :levels].set(mixing)
    group = TILE
    air_spec = pl.BlockSpec(
        (2, levels, group, cols), lambda i, flag: (0, 0, i * flag[0], 0)
    )
    phys = pl.pallas_call(
        physics_kernel,
        grid_spec=pltpu.PrefetchScalarGridSpec(
            num_scalar_prefetch=1,
            grid=(rows // group,),
            in_specs=[whole((depth, depth)), air_spec],
            out_specs=air_spec,
            scratch_shapes=[pltpu.VMEM((group, depth, cols), F32)] * 2,
        ),
        out_shape=jax.ShapeDtypeStruct(air_state.shape, F32),
        compiler_params=pltpu.CompilerParams(vmem_limit_bytes=32 * 2**20),
        cost_estimate=pl.CostEstimate(
            flops=2 * SUBSTEPS * rows * cols * depth * depth * 6,
            bytes_accessed=16 * levels * rows * cols,
            transcendentals=2 * SUBSTEPS * rows * cols * depth,
        ),
        name="column_physics",
    )(flag, mix, air_state)

    phys_spec = pl.BlockSpec((chunk, rows, cols), lambda i, flag: (i * flag[0], 0, 0))
    result = pl.pallas_call(
        final_kernel,
        grid_spec=pltpu.PrefetchScalarGridSpec(
            num_scalar_prefetch=1,
            grid=(steps,),
            in_specs=[
                plane_spec, plane_spec, phys_spec, whole((rows, cols)),
                whole((rows, LANES)), whole((rows, LANES)),
                whole((row_slots, cols)), whole((row_slots, cols)),
            ],
            out_specs=plane_spec,
            scratch_shapes=[
                pltpu.VMEM((rows, cols), F32),
            ],
        ),
        out_shape=plane,
        compiler_params=pltpu.CompilerParams(vmem_limit_bytes=32 * 2**20),
        name="step_sum",
    )(flag, flat, summed, phys.reshape(planes, rows, cols), msum, *edges)
    return result.reshape(air_state.shape)


def solution(mesh):
    placed = (P(None, None, "fy", "fx"), P("fy", "fx"), P("fy", "fx"), P(), P("fy", "fx"))
    return jax.shard_map(
        body, mesh=mesh, in_specs=placed, out_specs=P(None, None, "fy", "fx"), check_vma=False
    )
```

```python
import functools

import jax
import jax.numpy as jnp
import numpy as np
from jax import lax
from jax.experimental import pallas as pl
from jax.experimental.pallas import tpu as pltpu
from jax.sharding import PartitionSpec as P

SUBSTEPS = 24
UNROLL = 12
LOG2E = float(np.log2(np.e))
LN2 = float(np.log(2.0))
LANES = 128
TILE = 8
VMEM_LIMIT = 60 * 2**20
F32 = jnp.float32
BF16 = jnp.bfloat16


def gll_tables():
    nodes = np.array([-1.0, -1.0 / np.sqrt(5.0), 1.0 / np.sqrt(5.0), 1.0])
    gll_weight = np.array([1.0 / 6.0, 5.0 / 6.0, 5.0 / 6.0, 1.0 / 6.0])
    deriv = np.zeros((4, 4))
    for first in range(4):
        for second in range(4):
            if first == second:
                deriv[first, second] = sum(
                    (1.0 / (nodes[first] - nodes[other]) for other in range(4) if other != first)
                )
            else:
                top = np.prod([nodes[first] - nodes[other] for other in range(4) if other != first])
                below = np.prod(
                    [nodes[second] - nodes[other] for other in range(4) if other != second]
                )
                deriv[first, second] = top / below / (nodes[first] - nodes[second])
    stiff = deriv.T * gll_weight[None, :] @ deriv
    return (stiff, gll_weight)


def by_node(index, values):
    node = index % 4
    result = jnp.full(index.shape, values[0], F32)
    for k in range(1, 4):
        result = jnp.where(node == k, F32(values[k]), result)
    return result


def split(value):
    high = value.astype(BF16)
    low = (value - high.astype(F32)).astype(BF16)
    return high, low


def repeat(count, width, work):
    def several(k, _):
        for u in range(width):
            work(k * width + u)
        return 0

    lax.fori_loop(0, count // width, several, 0)
    for i in range(count // width * width, count):
        work(i)


def sum_cols(g):
    n = g.shape[-1]
    col = lax.broadcasted_iota(jnp.int32, g.shape, 1)
    upper = pltpu.roll(g, n - 1, 1)
    lower = pltpu.roll(g, 1, 1)
    up = (col % 4 == 3) & (col != n - 1)
    low = (col % 4 == 0) & (col != 0)
    return g + jnp.where(up, upper, jnp.where(low, lower, 0.0))


def sum_rows(g, first=0.0, last=0.0):
    n = g.shape[0]
    row = lax.broadcasted_iota(jnp.int32, g.shape, 0)
    upper = jnp.where(row == n - 1, last, pltpu.roll(g, n - 1, 0))
    lower = jnp.where(row == 0, first, pltpu.roll(g, 1, 0))
    return g + jnp.where(row % 4 == 3, upper, jnp.where(row % 4 == 0, lower, 0.0))


def node_rows(k, rows):
    return pl.ds(k, rows // 4, stride=4)


def local_kernel(*refs):
    halves = refs[-1].shape[0] // 4
    airs = refs[:halves]
    jac, visc, khi, klo, summed, msum, col_lo, col_hi, row_lo, row_hi = refs[halves : halves + 10]
    along, fa, fb, spread, out_lo, out_hi, _ = refs[halves + 10 :]
    step = pl.program_id(0)
    chunk, rows = airs[0].shape[:2]
    cols = jac.shape[1]
    elements = rows // 4
    stiff, weight = gll_tables()
    lane = lax.broadcasted_iota(jnp.int32, (elements, LANES), 1)
    element = lax.broadcasted_iota(jnp.int32, (elements, cols), 0)
    col = lax.broadcasted_iota(jnp.int32, (rows, cols), 1)
    up = (col % 4 == 3) & (col != cols - 1)
    low = (col % 4 == 0) & (col != 0)

    def put(ref, index, value):
        for h in range(halves):
            ref[h, index] = value[:, h * LANES : (h + 1) * LANES]

    def node_of(k, ref, *index):
        return jnp.concatenate(
            [ref[(h, *index, node_rows(k, rows), slice(None))] for h in range(halves)], axis=1
        )

    def keep_edges(nodes, index):
        mine = lane == index
        for k in range(4):
            value = nodes[k]
            out_lo[k] = jnp.where(mine, pltpu.roll(value[:, :LANES], index % LANES, 1), out_lo[k])
            out_hi[k] = jnp.where(
                mine, pltpu.roll(value[:, cols - LANES :], (index + 1) % LANES, 1), out_hi[k]
            )
        row_lo[pl.ds(index, 1), :] = nodes[0][0:1, :]
        row_hi[pl.ds(index, 1), :] = nodes[3][elements - 1 :, :]

    def sums(nodes):
        g = jnp.concatenate(nodes, axis=0)
        g = g + jnp.where(
            up, pltpu.roll(g, cols - 1, 1), jnp.where(low, pltpu.roll(g, 1, 1), 0.0)
        )
        g = [g[k * elements : (k + 1) * elements] for k in range(4)]
        before = jnp.where(element == 0, 0.0, pltpu.roll(g[3], 1, 0))
        after = jnp.where(element == elements - 1, 0.0, pltpu.roll(g[0], elements - 1, 0))
        return [g[0] + before, g[1], g[2], g[3] + after]

    def put_nodes(ref, index, nodes):
        for k in range(4):
            for h in range(halves):
                part = nodes[k][:, h * LANES : (h + 1) * LANES]
                ref[(h, *index, node_rows(k, rows), slice(None))] = part

    @pl.when(step == 0)
    def _():
        r = lax.broadcasted_iota(jnp.int32, (rows, cols), 0)
        mass = jac[...] * (by_node(r, weight) * by_node(col, weight))
        out_lo[...] = jnp.zeros_like(out_lo)
        out_hi[...] = jnp.zeros_like(out_hi)
        row_lo[...] = jnp.zeros_like(row_lo)
        row_hi[...] = jnp.zeros_like(row_hi)
        wide = by_node(col[:elements], weight)
        put(spread, 0, mass)
        put(spread, 1, visc[...])
        for k in range(4):
            minus = -node_of(k, spread, 1)
            fa[k] = minus * F32(weight[k])
            fb[k] = minus * wide
        nodes = [node_of(k, spread, 0) for k in range(4)]
        keep_edges(nodes, pl.num_programs(0) * chunk)
        put_nodes(msum, (), sums(nodes))

    state = jnp.concatenate([ref[...].reshape(chunk * rows, LANES) for ref in airs], axis=1)
    high, low_part = split(state)
    term = (
        jnp.dot(high, khi[...], preferred_element_type=F32)
        + jnp.dot(low_part, khi[...], preferred_element_type=F32)
        + jnp.dot(high, klo[...], preferred_element_type=F32)
    )
    for h in range(halves):
        along[h] = term[:, h * LANES : (h + 1) * LANES].reshape(chunk, rows, LANES)

    def level(i):
        f = [
            jnp.concatenate([ref[i, node_rows(k, rows), :] for ref in airs], axis=1)
            for k in range(4)
        ]
        nodes = []
        for k in range(4):
            across = F32(stiff[k, 0]) * f[0]
            for m in range(1, 4):
                across = across + F32(stiff[k, m]) * f[m]
            nodes.append(fa[k] * node_of(k, along, i) + fb[k] * across)
        keep_edges(nodes, step * chunk + i)
        put_nodes(summed, (i,), sums(nodes))

    repeat(chunk, 4, level)

    @pl.when(step == pl.num_programs(0) - 1)
    def _():
        for k in range(4):
            col_lo[node_rows(k, rows), :] = out_lo[k]
            col_hi[node_rows(k, rows), :] = out_hi[k]


def softplus2(y):
    return jnp.maximum(y, jnp.log2(1.0 + jnp.exp2(jnp.minimum(y, 100.0))))


def edge_kernel(
    nx, ny, col_lo, col_hi, row_lo, row_hi, edge_l, edge_r, edge_b, edge_a,
    cols_in, rows_in, corners_in, send, recv,
):
    rows = col_lo.shape[0]
    x, y = lax.axis_index("fx"), lax.axis_index("fy")
    west, east = lax.rem(x + nx - 1, nx), lax.rem(x + 1, nx)
    south, north = lax.rem(y + ny - 1, ny), lax.rem(y + 1, ny)
    around = [
        (west, y), (east, y), (x, south), (x, north),
        (west, south), (west, north), (east, south), (east, north),
    ]
    barrier = pltpu.get_barrier_semaphore()
    for device in around:
        pl.semaphore_signal(
            barrier, inc=1, device_id=device, device_id_type=pl.DeviceIdType.MESH
        )
    pl.semaphore_wait(barrier, len(around))
    first, last = pl.ds(0, TILE), pl.ds(rows - TILE, TILE)
    moves = [
        (row_hi, rows_in.at[0], around[3]),
        (row_lo, rows_in.at[1], around[2]),
        (col_hi, cols_in.at[0], around[1]),
        (col_lo, cols_in.at[1], around[0]),
        (col_hi.at[last], corners_in.at[0], around[7]),
        (col_hi.at[first], corners_in.at[1], around[6]),
        (col_lo.at[last], corners_in.at[2], around[5]),
        (col_lo.at[first], corners_in.at[3], around[4]),
    ]
    copies = []
    for k, (source, target, device) in enumerate(moves):
        copy = pltpu.make_async_remote_copy(
            src_ref=source, dst_ref=target, send_sem=send.at[k], recv_sem=recv.at[k],
            device_id=device, device_id_type=pl.DeviceIdType.MESH,
        )
        copy.start()
        copies.append(copy)
    for copy in copies:
        copy.wait()
    edge_l[...] = sum_rows(cols_in[0], corners_in[0, TILE - 1 :, :], corners_in[1, :1, :])
    edge_r[...] = sum_rows(cols_in[1], corners_in[2, TILE - 1 :, :], corners_in[3, :1, :])
    edge_b[...] = sum_cols(rows_in[0])
    edge_a[...] = sum_cols(rows_in[1])


def column_kernel(
    dest, mixing, air, summed, msum, edge_l, edge_r, edge_b, edge_a, out,
    air_v, sum_v, out_v, y, csum, inv, air_sem, sum_sem, out_sem,
):
    planes, rows, cols = air.shape
    levels = planes // 2
    depth = y.shape[1]
    groups = rows // TILE
    halves = cols // LANES
    parts = sum_sem.shape[0]
    chunk = planes // parts
    heavy = dest[0] >= 0

    def air_copy(g):
        band = pl.ds(pl.multiple_of(g * TILE, TILE), TILE)
        return pltpu.make_async_copy(air.at[:, band, :], air_v.at[:, band, :], air_sem.at[g])

    def sum_copy(k):
        part = pl.ds(k * chunk, chunk)
        return pltpu.make_async_copy(summed.at[:, part], sum_v.at[:, part], sum_sem.at[k])

    def out_copy(k):
        part = pl.ds(k * chunk, chunk)
        return pltpu.make_async_copy(out_v.at[part], out.at[part], out_sem.at[k])

    for g in range(groups):
        air_copy(g).start()
    for k in range(parts):
        sum_copy(k).start()

    @pl.when(heavy)
    def _():
        eye = lax.broadcasted_iota(jnp.int32, (depth, depth), 0) == lax.broadcasted_iota(
            jnp.int32, (depth, depth), 1
        )
        pad = depth - levels
        mix = jnp.concatenate([mixing[...], jnp.zeros((levels, pad), F32)], axis=1)
        mix = jnp.concatenate([mix, jnp.zeros((pad, depth), F32)], axis=0)
        ahigh, alow = split(0.125 * mix + jnp.where(eye, 0.25, 0.0))
        acat = jnp.concatenate([ahigh, ahigh, alow], axis=1)
        mhigh, mlow = split(0.25 * mix)
        mcat = jnp.concatenate([mhigh, mhigh, mlow], axis=1)

        def group(g, carry):
            air_copy(g).wait()
            band = pl.ds(pl.multiple_of(g * TILE, TILE), TILE)
            t = air_v[:levels, band, :].astype(BF16).astype(F32)
            q = air_v[levels:, band, :].astype(BF16).astype(F32)
            x = (q - 0.5 * t) * LOG2E
            y[...] = jnp.zeros_like(y)
            csum[...] = jnp.zeros_like(csum)
            for r in range(TILE):
                y[r, :levels, :] = x[:, r, :]

            def substep(_, carry):
                for r in range(TILE):
                    value = y[r]
                    cond = softplus2(value)
                    csum[r] += cond
                    high, low = split(cond)
                    stack = jnp.concatenate([high, low, high], axis=0)
                    y[r] = value - jnp.dot(acat, stack, preferred_element_type=F32)
                return carry

            lax.fori_loop(0, SUBSTEPS, substep, 0, unroll=UNROLL)
            for r in range(TILE):
                total = csum[r] * LN2
                high, low = split(total)
                stack = jnp.concatenate([high, low, high], axis=0)
                heat = jnp.dot(mcat, stack, preferred_element_type=F32)
                out_v[:levels, g * TILE + r, :] = heat[:levels]
                out_v[levels:, g * TILE + r, :] = -0.25 * total[:levels]
            return carry

        lax.fori_loop(0, groups, group, 0)

    @pl.when(jnp.logical_not(heavy))
    def _():
        for g in range(groups):
            air_copy(g).wait()

    row = lax.broadcasted_iota(jnp.int32, (TILE, cols), 0)
    lane = lax.broadcasted_iota(jnp.int32, (rows, LANES), 1)

    def full(base, index):
        west = pltpu.roll(edge_l[...], (LANES - index) % LANES, 1)
        east = pltpu.roll(edge_r[...], (2 * LANES - 1 - index) % LANES, 1)
        pieces = list(base)
        pieces[0] = pieces[0] + jnp.where(lane == 0, west, 0.0)
        pieces[-1] = pieces[-1] + jnp.where(lane == LANES - 1, east, 0.0)
        base = jnp.concatenate(pieces, axis=1)
        top = base[:TILE] + jnp.where(row == 0, edge_b[pl.ds(index, 1), :], 0.0)
        end = base[rows - TILE :] + jnp.where(row == TILE - 1, edge_a[pl.ds(index, 1), :], 0.0)
        return jnp.concatenate([top, base[TILE : rows - TILE], end], axis=0)

    inv[...] = 0.05 / full([msum[h] for h in range(halves)], planes)

    def finish(extra):
        for k in range(parts):
            sum_copy(k).wait()

            def level(i):
                index = k * chunk + i
                value = air_v[index] + inv[...] * full([sum_v[h, index] for h in range(halves)], index)
                if extra:
                    value = value + out_v[index]
                out_v[index] = value

            repeat(chunk, 4, level)
            out_copy(k).start()
        for k in range(parts):
            out_copy(k).wait()

    @pl.when(heavy)
    def _():
        finish(True)

    @pl.when(jnp.logical_not(heavy))
    def _():
        finish(False)


def body(air_state, jacobian, viscosity, mixing, convect_dest):
    _, levels, rows, cols = air_state.shape
    planes = 2 * levels
    chunk = levels // 2
    steps = planes // chunk
    flat = air_state.reshape(planes, rows, cols)
    stiff, _ = gll_tables()
    along_mat = np.kron(np.eye(cols // 4), stiff).astype(np.float32)
    khi = along_mat.astype(jnp.bfloat16)
    klo = (along_mat - khi.astype(np.float32)).astype(jnp.bfloat16)
    row_slots = -(-(planes + 1) // TILE) * TILE
    row_slots = -(-(planes + 1) // TILE) * TILE
    across_mat = np.kron(np.eye(rows // 4), stiff).astype(np.float32)
    across_hi = across_mat.astype(jnp.bfloat16)
    across_lo = (across_mat - across_hi.astype(np.float32)).astype(jnp.bfloat16)
    kacross = np.concatenate([across_hi, across_hi, across_lo], axis=1)

    def whole(shape):
        return pl.BlockSpec(shape, lambda *_: (0,) * len(shape))

    plane_spec = pl.BlockSpec((chunk, rows, cols), lambda i, *_: (i, 0, 0))
    plane = jax.ShapeDtypeStruct((planes, rows, cols), F32)
    edge_col = jax.ShapeDtypeStruct((rows, LANES), F32)
    edge_row = jax.ShapeDtypeStruct((row_slots, cols), F32)
    halves = cols // LANES
    elements = rows // 4

    def half_spec(h):
        return pl.BlockSpec((chunk, rows, LANES), lambda i: (i, 0, h))

    summed, msum, col_lo, col_hi, row_lo, row_hi = pl.pallas_call(
        local_kernel,
        grid=(steps,),
        out_shape=[
            jax.ShapeDtypeStruct((halves, planes, rows, LANES), F32),
            jax.ShapeDtypeStruct((halves, rows, LANES), F32),
            edge_col, edge_col, edge_row, edge_row,
        ],
        in_specs=[half_spec(h) for h in range(halves)]
        + [whole((rows, cols))] * 2 + [whole((cols, cols))] * 2,
        out_specs=[
            pl.BlockSpec((halves, chunk, rows, LANES), lambda i: (0, i, 0, 0)),
            whole((halves, rows, LANES)), whole((rows, LANES)), whole((rows, LANES)),
            whole((row_slots, cols)), whole((row_slots, cols)),
        ],
        scratch_shapes=[
            pltpu.VMEM((halves, chunk, rows, LANES), F32),
            pltpu.VMEM((4, elements, cols), F32),
            pltpu.VMEM((4, elements, cols), F32),
            pltpu.VMEM((halves, 2, rows, LANES), F32),
            pltpu.VMEM((4, elements, LANES), F32),
            pltpu.VMEM((4, elements, LANES), F32),
            pltpu.VMEM((4 * halves, LANES), F32),
        ],
        compiler_params=pltpu.CompilerParams(vmem_limit_bytes=VMEM_LIMIT),
        name="local_terms",
    )(*[flat] * halves, jacobian, viscosity, khi, klo)

    nx, ny = lax.axis_size("fx"), lax.axis_size("fy")

    vmem = pl.BlockSpec(memory_space=pltpu.VMEM)
    edges = pl.pallas_call(
        functools.partial(edge_kernel, nx, ny),
        out_shape=[edge_col, edge_col, edge_row, edge_row],
        in_specs=[vmem] * 4,
        out_specs=[vmem] * 4,
        scratch_shapes=[
            pltpu.VMEM((2, rows, LANES), F32),
            pltpu.VMEM((2, row_slots, cols), F32),
            pltpu.VMEM((4, TILE, LANES), F32),
            pltpu.SemaphoreType.DMA((8,)),
            pltpu.SemaphoreType.DMA((8,)),
        ],
        compiler_params=pltpu.CompilerParams(collective_id=0, has_side_effects=True, vmem_limit_bytes=VMEM_LIMIT),
        name="edge_exchange",
    )(col_lo, col_hi, row_lo, row_hi)

    depth = -(-levels // 16) * 16
    parts = 4
    anywhere = pl.BlockSpec(memory_space=pl.ANY)
    result = pl.pallas_call(
        column_kernel,
        out_shape=plane,
        in_specs=[pl.BlockSpec(memory_space=pltpu.SMEM), vmem] + [anywhere] * 2 + [vmem] * 5,
        out_specs=anywhere,
        scratch_shapes=[
            pltpu.VMEM((planes, rows, cols), F32),
            pltpu.VMEM((halves, planes, rows, LANES), F32),
            pltpu.VMEM((planes, rows, cols), F32),
            pltpu.VMEM((TILE, depth, cols), F32),
            pltpu.VMEM((TILE, depth, cols), F32),
            pltpu.VMEM((rows, cols), F32),
            pltpu.SemaphoreType.DMA((rows // TILE,)),
            pltpu.SemaphoreType.DMA((parts,)),
            pltpu.SemaphoreType.DMA((parts,)),
        ],
        compiler_params=pltpu.CompilerParams(vmem_limit_bytes=VMEM_LIMIT),
        name="column_step",
    )(convect_dest.reshape(rows), mixing, flat, summed, msum, *edges)
    return result.reshape(air_state.shape)


def solution(mesh):
    placed = (P(None, None, "fy", "fx"), P("fy", "fx"), P("fy", "fx"), P(), P("fy", "fx"))
    return jax.shard_map(
        body, mesh=mesh, in_specs=placed, out_specs=P(None, None, "fy", "fx"), check_vma=False
    )
```

```python
import functools

import jax
import jax.numpy as jnp
import numpy as np
from jax import lax
from jax.experimental import pallas as pl
from jax.experimental.pallas import tpu as pltpu
from jax.sharding import PartitionSpec as P

SUBSTEPS = 24
UNROLL = 23
LOG2E = float(np.log2(np.e))
LN2 = float(np.log(2.0))
LANES = 128
TILE = 8
VMEM_LIMIT = 60 * 2**20
F32 = jnp.float32
BF16 = jnp.bfloat16


def gll_tables():
    nodes = np.array([-1.0, -1.0 / np.sqrt(5.0), 1.0 / np.sqrt(5.0), 1.0])
    gll_weight = np.array([1.0 / 6.0, 5.0 / 6.0, 5.0 / 6.0, 1.0 / 6.0])
    deriv = np.zeros((4, 4))
    for first in range(4):
        for second in range(4):
            if first == second:
                deriv[first, second] = sum(
                    (1.0 / (nodes[first] - nodes[other]) for other in range(4) if other != first)
                )
            else:
                top = np.prod([nodes[first] - nodes[other] for other in range(4) if other != first])
                below = np.prod(
                    [nodes[second] - nodes[other] for other in range(4) if other != second]
                )
                deriv[first, second] = top / below / (nodes[first] - nodes[second])
    stiff = deriv.T * gll_weight[None, :] @ deriv
    return (stiff, gll_weight)


def by_node(index, values):
    node = index % 4
    result = jnp.full(index.shape, values[0], F32)
    for k in range(1, 4):
        result = jnp.where(node == k, F32(values[k]), result)
    return result


def split(value):
    high = value.astype(BF16)
    low = (value - high.astype(F32)).astype(BF16)
    return high, low


def repeat(count, width, work):
    def several(k, _):
        for u in range(width):
            work(k * width + u)
        return 0

    lax.fori_loop(0, count // width, several, 0)
    for i in range(count // width * width, count):
        work(i)


def sum_cols(g):
    n = g.shape[-1]
    col = lax.broadcasted_iota(jnp.int32, g.shape, 1)
    upper = pltpu.roll(g, n - 1, 1)
    lower = pltpu.roll(g, 1, 1)
    up = (col % 4 == 3) & (col != n - 1)
    low = (col % 4 == 0) & (col != 0)
    return g + jnp.where(up, upper, jnp.where(low, lower, 0.0))


def sum_rows(g, first=0.0, last=0.0):
    n = g.shape[0]
    row = lax.broadcasted_iota(jnp.int32, g.shape, 0)
    upper = jnp.where(row == n - 1, last, pltpu.roll(g, n - 1, 0))
    lower = jnp.where(row == 0, first, pltpu.roll(g, 1, 0))
    return g + jnp.where(row % 4 == 3, upper, jnp.where(row % 4 == 0, lower, 0.0))


def node_rows(k, rows):
    return pl.ds(k, rows // 4, stride=4)


def neighbours(nx, ny):
    x, y = lax.axis_index("fx"), lax.axis_index("fy")
    west, east = lax.rem(x + nx - 1, nx), lax.rem(x + 1, nx)
    south, north = lax.rem(y + ny - 1, ny), lax.rem(y + 1, ny)
    return [
        (west, y), (east, y), (x, south), (x, north),
        (west, south), (west, north), (east, south), (east, north),
    ]


def local_kernel(nx, ny, halves, *refs):
    airs = refs[:halves]
    jac, visc, khi, klo, summed, msum, edge_l, edge_r, edge_b, edge_a = refs[halves : halves + 10]
    along, fa, fb, spread, out_lo, out_hi, col_lo, col_hi, row_lo, row_hi = refs[
        halves + 10 : halves + 20
    ]
    cols_in, rows_in, corners_in, send, recv = refs[halves + 20 :]
    around = neighbours(nx, ny)
    step = pl.program_id(0)
    chunk, rows = airs[0].shape[:2]
    cols = jac.shape[1]
    elements = rows // 4
    stiff, weight = gll_tables()
    lane = lax.broadcasted_iota(jnp.int32, (elements, LANES), 1)
    element = lax.broadcasted_iota(jnp.int32, (elements, cols), 0)
    col = lax.broadcasted_iota(jnp.int32, (rows, cols), 1)
    up = (col % 4 == 3) & (col != cols - 1)
    low = (col % 4 == 0) & (col != 0)

    def put(ref, index, value):
        for h in range(halves):
            ref[h, index] = value[:, h * LANES : (h + 1) * LANES]

    def node_of(k, ref, *index):
        return jnp.concatenate(
            [ref[(h, *index, node_rows(k, rows), slice(None))] for h in range(halves)], axis=1
        )

    def keep_edges(nodes, index):
        mine = lane == index
        for k in range(4):
            value = nodes[k]
            out_lo[k] = jnp.where(mine, pltpu.roll(value[:, :LANES], index % LANES, 1), out_lo[k])
            out_hi[k] = jnp.where(
                mine, pltpu.roll(value[:, cols - LANES :], (index + 1) % LANES, 1), out_hi[k]
            )
        row_lo[pl.ds(index, 1), :] = nodes[0][0:1, :]
        row_hi[pl.ds(index, 1), :] = nodes[3][elements - 1 :, :]

    def sums(nodes):
        g = jnp.concatenate(nodes, axis=0)
        g = g + jnp.where(
            up, pltpu.roll(g, cols - 1, 1), jnp.where(low, pltpu.roll(g, 1, 1), 0.0)
        )
        g = [g[k * elements : (k + 1) * elements] for k in range(4)]
        before = jnp.where(element == 0, 0.0, pltpu.roll(g[3], 1, 0))
        after = jnp.where(element == elements - 1, 0.0, pltpu.roll(g[0], elements - 1, 0))
        return [g[0] + before, g[1], g[2], g[3] + after]

    def put_nodes(ref, index, nodes):
        for k in range(4):
            for h in range(halves):
                part = nodes[k][:, h * LANES : (h + 1) * LANES]
                ref[(h, *index, node_rows(k, rows), slice(None))] = part

    @pl.when(step == 0)
    def _():
        barrier = pltpu.get_barrier_semaphore()
        for device in around:
            pl.semaphore_signal(
                barrier, inc=1, device_id=device, device_id_type=pl.DeviceIdType.MESH
            )
        r = lax.broadcasted_iota(jnp.int32, (rows, cols), 0)
        mass = jac[...] * (by_node(r, weight) * by_node(col, weight))
        out_lo[...] = jnp.zeros_like(out_lo)
        out_hi[...] = jnp.zeros_like(out_hi)
        row_lo[...] = jnp.zeros_like(row_lo)
        row_hi[...] = jnp.zeros_like(row_hi)
        wide = by_node(col[:elements], weight)
        put(spread, 0, mass)
        put(spread, 1, visc[...])
        for k in range(4):
            minus = -node_of(k, spread, 1)
            fa[k] = minus * F32(weight[k])
            fb[k] = minus * wide
        nodes = [node_of(k, spread, 0) for k in range(4)]
        keep_edges(nodes, pl.num_programs(0) * chunk)
        put_nodes(msum, (), sums(nodes))

    state = jnp.concatenate([ref[...].reshape(chunk * rows, LANES) for ref in airs], axis=1)
    high, low_part = split(state)
    term = (
        jnp.dot(high, khi[...], preferred_element_type=F32)
        + jnp.dot(low_part, khi[...], preferred_element_type=F32)
        + jnp.dot(high, klo[...], preferred_element_type=F32)
    )
    for h in range(halves):
        along[h] = term[:, h * LANES : (h + 1) * LANES].reshape(chunk, rows, LANES)

    def level(i):
        f = [
            jnp.concatenate([ref[i, node_rows(k, rows), :] for ref in airs], axis=1)
            for k in range(4)
        ]
        nodes = []
        for k in range(4):
            across = F32(stiff[k, 0]) * f[0]
            for m in range(1, 4):
                across = across + F32(stiff[k, m]) * f[m]
            nodes.append(fa[k] * node_of(k, along, i) + fb[k] * across)
        keep_edges(nodes, step * chunk + i)
        put_nodes(summed, (i,), sums(nodes))

    repeat(chunk, 4, level)

    @pl.when(step == pl.num_programs(0) - 1)
    def _():
        for k in range(4):
            col_lo[node_rows(k, rows), :] = out_lo[k]
            col_hi[node_rows(k, rows), :] = out_hi[k]
        pl.semaphore_wait(pltpu.get_barrier_semaphore(), len(around))
        first, last = pl.ds(0, TILE), pl.ds(rows - TILE, TILE)
        moves = [
            (row_hi, rows_in.at[0], around[3]),
            (row_lo, rows_in.at[1], around[2]),
            (col_hi, cols_in.at[0], around[1]),
            (col_lo, cols_in.at[1], around[0]),
            (col_hi.at[last], corners_in.at[0], around[7]),
            (col_hi.at[first], corners_in.at[1], around[6]),
            (col_lo.at[last], corners_in.at[2], around[5]),
            (col_lo.at[first], corners_in.at[3], around[4]),
        ]
        copies = []
        for k, (source, target, device) in enumerate(moves):
            copy = pltpu.make_async_remote_copy(
                src_ref=source, dst_ref=target, send_sem=send.at[k], recv_sem=recv.at[k],
                device_id=device, device_id_type=pl.DeviceIdType.MESH,
            )
            copy.start()
            copies.append(copy)
        for copy in copies:
            copy.wait()
        edge_l[...] = sum_rows(cols_in[0], corners_in[0, TILE - 1 :, :], corners_in[1, :1, :])
        edge_r[...] = sum_rows(cols_in[1], corners_in[2, TILE - 1 :, :], corners_in[3, :1, :])
        edge_b[...] = sum_cols(rows_in[0])
        edge_a[...] = sum_cols(rows_in[1])


def softplus2(y):
    return jnp.maximum(y, jnp.log2(1.0 + jnp.exp2(jnp.minimum(y, 100.0))))


def column_kernel(
    dest, mixing, air, summed, msum, edge_l, edge_r, edge_b, edge_a, out,
    air_v, sum_v, out_v, y, csum, inv, air_sem, sum_sem, out_sem,
):
    planes, rows, cols = air.shape
    levels = planes // 2
    depth = y.shape[1]
    groups = rows // TILE
    halves = cols // LANES
    parts = sum_sem.shape[0]
    chunk = planes // parts
    heavy = dest[0] >= 0

    def air_copy(g):
        band = pl.ds(pl.multiple_of(g * TILE, TILE), TILE)
        return pltpu.make_async_copy(air.at[:, band, :], air_v.at[:, band, :], air_sem.at[g])

    def sum_copy(k):
        part = pl.ds(k * chunk, chunk)
        return pltpu.make_async_copy(summed.at[:, part], sum_v.at[:, part], sum_sem.at[k])

    def out_copy(k):
        part = pl.ds(k * chunk, chunk)
        return pltpu.make_async_copy(out_v.at[part], out.at[part], out_sem.at[k])

    for g in range(groups):
        air_copy(g).start()
    for k in range(parts):
        sum_copy(k).start()

    @pl.when(heavy)
    def _():
        eye = lax.broadcasted_iota(jnp.int32, (depth, depth), 0) == lax.broadcasted_iota(
            jnp.int32, (depth, depth), 1
        )
        pad = depth - levels
        mix = jnp.concatenate([mixing[...], jnp.zeros((levels, pad), F32)], axis=1)
        mix = jnp.concatenate([mix, jnp.zeros((pad, depth), F32)], axis=0)
        ahigh, alow = split(0.125 * mix + jnp.where(eye, 0.25, 0.0))
        acat = jnp.concatenate([ahigh, ahigh, alow], axis=1)
        mhigh, mlow = split(0.25 * mix)
        mcat = jnp.concatenate([mhigh, mhigh, mlow], axis=1)

        def group(g, carry):
            air_copy(g).wait()
            band = pl.ds(pl.multiple_of(g * TILE, TILE), TILE)
            t = air_v[:levels, band, :].astype(BF16).astype(F32)
            q = air_v[levels:, band, :].astype(BF16).astype(F32)
            x = (q - 0.5 * t) * LOG2E
            y[...] = jnp.zeros_like(y)
            for r in range(TILE):
                y[r, :levels, :] = x[:, r, :]
                csum[r] = softplus2(y[r])

            def substep(_, carry):
                for r in range(TILE):
                    total = csum[r]
                    high, low = split(total)
                    stack = jnp.concatenate([high, low, high], axis=0)
                    value = y[r] - jnp.dot(acat, stack, preferred_element_type=F32)
                    csum[r] = total + softplus2(value)
                return carry

            lax.fori_loop(0, SUBSTEPS - 1, substep, 0, unroll=UNROLL)
            for r in range(TILE):
                total = csum[r] * LN2
                high, low = split(total)
                stack = jnp.concatenate([high, low, high], axis=0)
                heat = jnp.dot(mcat, stack, preferred_element_type=F32)
                out_v[:levels, g * TILE + r, :] = heat[:levels]
                out_v[levels:, g * TILE + r, :] = -0.25 * total[:levels]
            return carry

        lax.fori_loop(0, groups, group, 0)

    @pl.when(jnp.logical_not(heavy))
    def _():
        for g in range(groups):
            air_copy(g).wait()

    row = lax.broadcasted_iota(jnp.int32, (TILE, cols), 0)
    lane = lax.broadcasted_iota(jnp.int32, (rows, LANES), 1)

    def full(base, index):
        west = pltpu.roll(edge_l[...], (LANES - index) % LANES, 1)
        east = pltpu.roll(edge_r[...], (2 * LANES - 1 - index) % LANES, 1)
        pieces = list(base)
        pieces[0] = pieces[0] + jnp.where(lane == 0, west, 0.0)
        pieces[-1] = pieces[-1] + jnp.where(lane == LANES - 1, east, 0.0)
        base = jnp.concatenate(pieces, axis=1)
        top = base[:TILE] + jnp.where(row == 0, edge_b[pl.ds(index, 1), :], 0.0)
        end = base[rows - TILE :] + jnp.where(row == TILE - 1, edge_a[pl.ds(index, 1), :], 0.0)
        return jnp.concatenate([top, base[TILE : rows - TILE], end], axis=0)

    inv[...] = 0.05 / full([msum[h] for h in range(halves)], planes)

    def finish(extra):
        for k in range(parts):
            sum_copy(k).wait()

            def level(i):
                index = k * chunk + i
                value = air_v[index] + inv[...] * full([sum_v[h, index] for h in range(halves)], index)
                if extra:
                    value = value + out_v[index]
                out_v[index] = value

            repeat(chunk, 4, level)
            out_copy(k).start()
        for k in range(parts):
            out_copy(k).wait()

    @pl.when(heavy)
    def _():
        finish(True)

    @pl.when(jnp.logical_not(heavy))
    def _():
        finish(False)


def body(air_state, jacobian, viscosity, mixing, convect_dest):
    _, levels, rows, cols = air_state.shape
    planes = 2 * levels
    chunk = levels // 2
    steps = planes // chunk
    flat = air_state.reshape(planes, rows, cols)
    stiff, _ = gll_tables()
    along_mat = np.kron(np.eye(cols // 4), stiff).astype(np.float32)
    khi = along_mat.astype(jnp.bfloat16)
    klo = (along_mat - khi.astype(np.float32)).astype(jnp.bfloat16)
    row_slots = -(-(planes + 1) // TILE) * TILE
    row_slots = -(-(planes + 1) // TILE) * TILE
    across_mat = np.kron(np.eye(rows // 4), stiff).astype(np.float32)
    across_hi = across_mat.astype(jnp.bfloat16)
    across_lo = (across_mat - across_hi.astype(np.float32)).astype(jnp.bfloat16)
    kacross = np.concatenate([across_hi, across_hi, across_lo], axis=1)

    def whole(shape):
        return pl.BlockSpec(shape, lambda *_: (0,) * len(shape))

    plane_spec = pl.BlockSpec((chunk, rows, cols), lambda i, *_: (i, 0, 0))
    plane = jax.ShapeDtypeStruct((planes, rows, cols), F32)
    edge_col = jax.ShapeDtypeStruct((rows, LANES), F32)
    edge_row = jax.ShapeDtypeStruct((row_slots, cols), F32)
    halves = cols // LANES
    elements = rows // 4

    def half_spec(h):
        return pl.BlockSpec((chunk, rows, LANES), lambda i: (i, 0, h))

    nx, ny = lax.axis_size("fx"), lax.axis_size("fy")
    summed, msum, *edges = pl.pallas_call(
        functools.partial(local_kernel, nx, ny, halves),
        grid=(steps,),
        out_shape=[
            jax.ShapeDtypeStruct((halves, planes, rows, LANES), F32),
            jax.ShapeDtypeStruct((halves, rows, LANES), F32),
            edge_col, edge_col, edge_row, edge_row,
        ],
        in_specs=[half_spec(h) for h in range(halves)]
        + [whole((rows, cols))] * 2 + [whole((cols, cols))] * 2,
        out_specs=[
            pl.BlockSpec((halves, chunk, rows, LANES), lambda i: (0, i, 0, 0)),
            whole((halves, rows, LANES)), whole((rows, LANES)), whole((rows, LANES)),
            whole((row_slots, cols)), whole((row_slots, cols)),
        ],
        scratch_shapes=[
            pltpu.VMEM((halves, chunk, rows, LANES), F32),
            pltpu.VMEM((4, elements, cols), F32),
            pltpu.VMEM((4, elements, cols), F32),
            pltpu.VMEM((halves, 2, rows, LANES), F32),
            pltpu.VMEM((4, elements, LANES), F32),
            pltpu.VMEM((4, elements, LANES), F32),
            pltpu.VMEM((rows, LANES), F32),
            pltpu.VMEM((rows, LANES), F32),
            pltpu.VMEM((row_slots, cols), F32),
            pltpu.VMEM((row_slots, cols), F32),
            pltpu.VMEM((2, rows, LANES), F32),
            pltpu.VMEM((2, row_slots, cols), F32),
            pltpu.VMEM((4, TILE, LANES), F32),
            pltpu.SemaphoreType.DMA((8,)),
            pltpu.SemaphoreType.DMA((8,)),
        ],
        compiler_params=pltpu.CompilerParams(
            collective_id=0, has_side_effects=True, vmem_limit_bytes=VMEM_LIMIT
        ),
        name="local_terms",
    )(*[flat] * halves, jacobian, viscosity, khi, klo)

    vmem = pl.BlockSpec(memory_space=pltpu.VMEM)
    depth = -(-levels // 16) * 16
    parts = 4
    anywhere = pl.BlockSpec(memory_space=pl.ANY)
    result = pl.pallas_call(
        column_kernel,
        out_shape=plane,
        in_specs=[pl.BlockSpec(memory_space=pltpu.SMEM), vmem] + [anywhere] * 2 + [vmem] * 5,
        out_specs=anywhere,
        scratch_shapes=[
            pltpu.VMEM((planes, rows, cols), F32),
            pltpu.VMEM((halves, planes, rows, LANES), F32),
            pltpu.VMEM((planes, rows, cols), F32),
            pltpu.VMEM((TILE, depth, cols), F32),
            pltpu.VMEM((TILE, depth, cols), F32),
            pltpu.VMEM((rows, cols), F32),
            pltpu.SemaphoreType.DMA((rows // TILE,)),
            pltpu.SemaphoreType.DMA((parts,)),
            pltpu.SemaphoreType.DMA((parts,)),
        ],
        compiler_params=pltpu.CompilerParams(vmem_limit_bytes=VMEM_LIMIT),
        name="column_step",
    )(convect_dest.reshape(rows), mixing, flat, summed, msum, *edges)
    return result.reshape(air_state.shape)


def solution(mesh):
    placed = (P(None, None, "fy", "fx"), P("fy", "fx"), P("fy", "fx"), P(), P("fy", "fx"))
    return jax.shard_map(
        body, mesh=mesh, in_specs=placed, out_specs=P(None, None, "fy", "fx"), check_vma=False
    )
```

```python
import functools

import jax
import jax.numpy as jnp
import numpy as np
from jax import lax
from jax.experimental import pallas as pl
from jax.experimental.pallas import tpu as pltpu
from jax.sharding import PartitionSpec as P

SUBSTEPS = 24
UNROLL = 23
LOG2E = float(np.log2(np.e))
LN2 = float(np.log(2.0))
LANES = 128
TILE = 8
VMEM_LIMIT = 60 * 2**20
F32 = jnp.float32
BF16 = jnp.bfloat16


def gll_tables():
    nodes = np.array([-1.0, -1.0 / np.sqrt(5.0), 1.0 / np.sqrt(5.0), 1.0])
    gll_weight = np.array([1.0 / 6.0, 5.0 / 6.0, 5.0 / 6.0, 1.0 / 6.0])
    deriv = np.zeros((4, 4))
    for first in range(4):
        for second in range(4):
            if first == second:
                deriv[first, second] = sum(
                    (1.0 / (nodes[first] - nodes[other]) for other in range(4) if other != first)
                )
            else:
                top = np.prod([nodes[first] - nodes[other] for other in range(4) if other != first])
                below = np.prod(
                    [nodes[second] - nodes[other] for other in range(4) if other != second]
                )
                deriv[first, second] = top / below / (nodes[first] - nodes[second])
    stiff = deriv.T * gll_weight[None, :] @ deriv
    return (stiff, gll_weight)


def by_node(index, values):
    node = index % 4
    result = jnp.full(index.shape, values[0], F32)
    for k in range(1, 4):
        result = jnp.where(node == k, F32(values[k]), result)
    return result


def split(value):
    high = value.astype(BF16)
    low = (value - high.astype(F32)).astype(BF16)
    return high, low


def repeat(count, width, work):
    def several(k, _):
        for u in range(width):
            work(k * width + u)
        return 0

    lax.fori_loop(0, count // width, several, 0)
    for i in range(count // width * width, count):
        work(i)


def sum_cols(g):
    n = g.shape[-1]
    col = lax.broadcasted_iota(jnp.int32, g.shape, 1)
    upper = pltpu.roll(g, n - 1, 1)
    lower = pltpu.roll(g, 1, 1)
    up = (col % 4 == 3) & (col != n - 1)
    low = (col % 4 == 0) & (col != 0)
    return g + jnp.where(up, upper, jnp.where(low, lower, 0.0))


def sum_rows(g, first=0.0, last=0.0):
    n = g.shape[0]
    row = lax.broadcasted_iota(jnp.int32, g.shape, 0)
    upper = jnp.where(row == n - 1, last, pltpu.roll(g, n - 1, 0))
    lower = jnp.where(row == 0, first, pltpu.roll(g, 1, 0))
    return g + jnp.where(row % 4 == 3, upper, jnp.where(row % 4 == 0, lower, 0.0))


def node_rows(k, rows):
    return pl.ds(k, rows // 4, stride=4)


def neighbours(nx, ny):
    x, y = lax.axis_index("fx"), lax.axis_index("fy")
    west, east = lax.rem(x + nx - 1, nx), lax.rem(x + 1, nx)
    south, north = lax.rem(y + ny - 1, ny), lax.rem(y + 1, ny)
    return [
        (west, y), (east, y), (x, south), (x, north),
        (west, south), (west, north), (east, south), (east, north),
    ]


def local_kernel(nx, ny, halves, *refs):
    airs = refs[:halves]
    jac, visc, khi, klo, summed, msum, edge_l, edge_r, edge_b, edge_a = refs[halves : halves + 10]
    along, fa, fb, spread, out_lo, out_hi, col_lo, col_hi, row_lo, row_hi = refs[
        halves + 10 : halves + 20
    ]
    cols_in, rows_in, corners_in, send, recv = refs[halves + 20 :]
    around = neighbours(nx, ny)
    step = pl.program_id(0)
    chunk, rows = airs[0].shape[:2]
    cols = jac.shape[1]
    elements = rows // 4
    stiff, weight = gll_tables()
    lane = lax.broadcasted_iota(jnp.int32, (elements, LANES), 1)
    element = lax.broadcasted_iota(jnp.int32, (elements, cols), 0)
    col = lax.broadcasted_iota(jnp.int32, (rows, cols), 1)
    up = (col % 4 == 3) & (col != cols - 1)
    low = (col % 4 == 0) & (col != 0)

    def put(ref, index, value):
        for h in range(halves):
            ref[h, index] = value[:, h * LANES : (h + 1) * LANES]

    def node_of(k, ref, *index):
        return jnp.concatenate(
            [ref[(h, *index, node_rows(k, rows), slice(None))] for h in range(halves)], axis=1
        )

    def keep_edges(nodes, index):
        mine = lane == index
        for k in range(4):
            value = nodes[k]
            out_lo[k] = jnp.where(mine, pltpu.roll(value[:, :LANES], index % LANES, 1), out_lo[k])
            out_hi[k] = jnp.where(
                mine, pltpu.roll(value[:, cols - LANES :], (index + 1) % LANES, 1), out_hi[k]
            )
        row_lo[pl.ds(index, 1), :] = nodes[0][0:1, :]
        row_hi[pl.ds(index, 1), :] = nodes[3][elements - 1 :, :]

    def sums(nodes):
        g = jnp.concatenate(nodes, axis=0)
        g = g + jnp.where(
            up, pltpu.roll(g, cols - 1, 1), jnp.where(low, pltpu.roll(g, 1, 1), 0.0)
        )
        g = [g[k * elements : (k + 1) * elements] for k in range(4)]
        before = jnp.where(element == 0, 0.0, pltpu.roll(g[3], 1, 0))
        after = jnp.where(element == elements - 1, 0.0, pltpu.roll(g[0], elements - 1, 0))
        return [g[0] + before, g[1], g[2], g[3] + after]

    def put_nodes(ref, index, nodes):
        for k in range(4):
            for h in range(halves):
                part = nodes[k][:, h * LANES : (h + 1) * LANES]
                ref[(h, *index, node_rows(k, rows), slice(None))] = part

    @pl.when(step == 0)
    def _():
        barrier = pltpu.get_barrier_semaphore()
        for device in around:
            pl.semaphore_signal(
                barrier, inc=1, device_id=device, device_id_type=pl.DeviceIdType.MESH
            )
        r = lax.broadcasted_iota(jnp.int32, (rows, cols), 0)
        mass = jac[...] * (by_node(r, weight) * by_node(col, weight))
        out_lo[...] = jnp.zeros_like(out_lo)
        out_hi[...] = jnp.zeros_like(out_hi)
        row_lo[...] = jnp.zeros_like(row_lo)
        row_hi[...] = jnp.zeros_like(row_hi)
        wide = by_node(col[:elements], weight)
        put(spread, 0, mass)
        put(spread, 1, visc[...])
        for k in range(4):
            minus = -node_of(k, spread, 1)
            fa[k] = minus * F32(weight[k])
            fb[k] = minus * wide
        nodes = [node_of(k, spread, 0) for k in range(4)]
        keep_edges(nodes, pl.num_programs(0) * chunk)
        put_nodes(msum, (), sums(nodes))

    state = jnp.concatenate([ref[...].reshape(chunk * rows, LANES) for ref in airs], axis=1)
    high, low_part = split(state)
    term = (
        jnp.dot(high, khi[...], preferred_element_type=F32)
        + jnp.dot(low_part, khi[...], preferred_element_type=F32)
        + jnp.dot(high, klo[...], preferred_element_type=F32)
    )
    for h in range(halves):
        along[h] = term[:, h * LANES : (h + 1) * LANES].reshape(chunk, rows, LANES)

    def level(i):
        f = [
            jnp.concatenate([ref[i, node_rows(k, rows), :] for ref in airs], axis=1)
            for k in range(4)
        ]
        nodes = []
        for k in range(4):
            across = F32(stiff[k, 0]) * f[0]
            for m in range(1, 4):
                across = across + F32(stiff[k, m]) * f[m]
            nodes.append(fa[k] * node_of(k, along, i) + fb[k] * across)
        keep_edges(nodes, step * chunk + i)
        put_nodes(summed, (i,), sums(nodes))

    repeat(chunk, 15, level)

    @pl.when(step == pl.num_programs(0) - 1)
    def _():
        for k in range(4):
            col_lo[node_rows(k, rows), :] = out_lo[k]
            col_hi[node_rows(k, rows), :] = out_hi[k]
        pl.semaphore_wait(pltpu.get_barrier_semaphore(), len(around))
        first, last = pl.ds(0, TILE), pl.ds(rows - TILE, TILE)
        moves = [
            (row_hi, rows_in.at[0], around[3]),
            (row_lo, rows_in.at[1], around[2]),
            (col_hi, cols_in.at[0], around[1]),
            (col_lo, cols_in.at[1], around[0]),
            (col_hi.at[last], corners_in.at[0], around[7]),
            (col_hi.at[first], corners_in.at[1], around[6]),
            (col_lo.at[last], corners_in.at[2], around[5]),
            (col_lo.at[first], corners_in.at[3], around[4]),
        ]
        copies = []
        for k, (source, target, device) in enumerate(moves):
            copy = pltpu.make_async_remote_copy(
                src_ref=source, dst_ref=target, send_sem=send.at[k], recv_sem=recv.at[k],
                device_id=device, device_id_type=pl.DeviceIdType.MESH,
            )
            copy.start()
            copies.append(copy)
        for copy in copies:
            copy.wait()
        edge_l[...] = sum_rows(cols_in[0], corners_in[0, TILE - 1 :, :], corners_in[1, :1, :])
        edge_r[...] = sum_rows(cols_in[1], corners_in[2, TILE - 1 :, :], corners_in[3, :1, :])
        edge_b[...] = sum_cols(rows_in[0])
        edge_a[...] = sum_cols(rows_in[1])


def softplus2(y):
    return jnp.maximum(y, jnp.log2(1.0 + jnp.exp2(jnp.minimum(y, 100.0))))


def column_kernel(
    dest, mixing, air, summed, *refs
):
    late, out = refs[:5], refs[5]
    air_v, sum_v, out_v, y, csum, inv, air_sem, sum_sem, out_sem, late_sem = refs[6:16]
    late_v = refs[16:]
    msum, edge_l, edge_r, edge_b, edge_a = late_v
    planes, groups, _, cols = air.shape
    rows = groups * TILE
    levels = planes // 2
    depth = y.shape[1]
    halves = cols // LANES
    parts = sum_sem.shape[0]
    chunk = planes // parts
    heavy = dest[0] >= 0

    def air_copy(g):
        return pltpu.make_async_copy(air.at[:, g], air_v.at[:, g], air_sem.at[g])

    def sum_copy(k):
        part = pl.ds(k * chunk, chunk)
        return pltpu.make_async_copy(summed.at[:, part], sum_v.at[:, part], sum_sem.at[k])

    def out_copy(k):
        part = pl.ds(k * chunk, chunk)
        return pltpu.make_async_copy(out_v.at[part], out.at[part], out_sem.at[k])

    def late_copy(k):
        return pltpu.make_async_copy(late[k], late_v[k], late_sem.at[k])

    def start_rest():
        for g in range(1, groups):
            air_copy(g).start()
        for k in range(len(late)):
            late_copy(k).start()
        for k in range(parts):
            sum_copy(k).start()

    air_copy(0).start()

    @pl.when(heavy)
    def _():
        eye = lax.broadcasted_iota(jnp.int32, (depth, depth), 0) == lax.broadcasted_iota(
            jnp.int32, (depth, depth), 1
        )
        pad = depth - levels
        mix = jnp.concatenate([mixing[...], jnp.zeros((levels, pad), F32)], axis=1)
        mix = jnp.concatenate([mix, jnp.zeros((pad, depth), F32)], axis=0)
        ahigh, alow = split(0.125 * mix + jnp.where(eye, 0.25, 0.0))
        acat = jnp.concatenate([ahigh, ahigh, alow], axis=1)
        mhigh, mlow = split(0.25 * mix)
        mcat = jnp.concatenate([mhigh, mhigh, mlow], axis=1)

        air_copy(0).wait()
        start_rest()

        def group(g, carry):
            @pl.when(g > 0)
            def _():
                air_copy(g).wait()

            t = air_v[:levels, g].astype(BF16).astype(F32)
            q = air_v[levels:, g].astype(BF16).astype(F32)
            x = (q - 0.5 * t) * LOG2E
            y[...] = jnp.zeros_like(y)
            for r in range(TILE):
                y[r, :levels, :] = x[:, r, :]
                csum[r] = softplus2(y[r])

            def substep(_, carry):
                for r in range(TILE):
                    total = csum[r]
                    high, low = split(total)
                    stack = jnp.concatenate([high, low, high], axis=0)
                    value = y[r] - jnp.dot(acat, stack, preferred_element_type=F32)
                    csum[r] = total + softplus2(value)
                return carry

            lax.fori_loop(0, SUBSTEPS - 1, substep, 0, unroll=UNROLL)
            for r in range(TILE):
                total = csum[r] * LN2
                high, low = split(total)
                stack = jnp.concatenate([high, low, high], axis=0)
                heat = jnp.dot(mcat, stack, preferred_element_type=F32)
                out_v[:levels, g, r, :] = heat[:levels]
                out_v[levels:, g, r, :] = -0.25 * total[:levels]
            return carry

        lax.fori_loop(0, groups, group, 0)

    @pl.when(jnp.logical_not(heavy))
    def _():
        start_rest()
        for g in range(groups):
            air_copy(g).wait()

    for k in range(len(late)):
        late_copy(k).wait()

    row = lax.broadcasted_iota(jnp.int32, (TILE, cols), 0)
    lane = lax.broadcasted_iota(jnp.int32, (rows, LANES), 1)

    def full(base, index):
        west = pltpu.roll(edge_l[...], (LANES - index) % LANES, 1)
        east = pltpu.roll(edge_r[...], (2 * LANES - 1 - index) % LANES, 1)
        pieces = list(base)
        pieces[0] = pieces[0] + jnp.where(lane == 0, west, 0.0)
        pieces[-1] = pieces[-1] + jnp.where(lane == LANES - 1, east, 0.0)
        base = jnp.concatenate(pieces, axis=1)
        top = base[:TILE] + jnp.where(row == 0, edge_b[pl.ds(index, 1), :], 0.0)
        end = base[rows - TILE :] + jnp.where(row == TILE - 1, edge_a[pl.ds(index, 1), :], 0.0)
        return jnp.concatenate([top, base[TILE : rows - TILE], end], axis=0)

    inv[...] = 0.05 / full([msum[h] for h in range(halves)], planes)

    def finish(extra):
        for k in range(parts):
            sum_copy(k).wait()

            def level(i):
                index = k * chunk + i
                value = air_v[index].reshape(rows, cols) + inv[...] * full([sum_v[h, index] for h in range(halves)], index)
                if extra:
                    value = value + out_v[index].reshape(rows, cols)
                out_v[index] = value.reshape(groups, TILE, cols)

            repeat(chunk, 15, level)
            out_copy(k).start()
        for k in range(parts):
            out_copy(k).wait()

    @pl.when(heavy)
    def _():
        finish(True)

    @pl.when(jnp.logical_not(heavy))
    def _():
        finish(False)


def body(air_state, jacobian, viscosity, mixing, convect_dest):
    _, levels, rows, cols = air_state.shape
    planes = 2 * levels
    chunk = levels // 2
    steps = planes // chunk
    flat = air_state.reshape(planes, rows, cols)
    stiff, _ = gll_tables()
    along_mat = np.kron(np.eye(cols // 4), stiff).astype(np.float32)
    khi = along_mat.astype(jnp.bfloat16)
    klo = (along_mat - khi.astype(np.float32)).astype(jnp.bfloat16)
    row_slots = -(-(planes + 1) // TILE) * TILE
    row_slots = -(-(planes + 1) // TILE) * TILE
    across_mat = np.kron(np.eye(rows // 4), stiff).astype(np.float32)
    across_hi = across_mat.astype(jnp.bfloat16)
    across_lo = (across_mat - across_hi.astype(np.float32)).astype(jnp.bfloat16)
    kacross = np.concatenate([across_hi, across_hi, across_lo], axis=1)

    def whole(shape):
        return pl.BlockSpec(shape, lambda *_: (0,) * len(shape))

    edge_col = jax.ShapeDtypeStruct((rows, LANES), F32)
    edge_row = jax.ShapeDtypeStruct((row_slots, cols), F32)
    halves = cols // LANES
    elements = rows // 4

    def half_spec(h):
        return pl.BlockSpec((chunk, rows, LANES), lambda i: (i, 0, h))

    nx, ny = lax.axis_size("fx"), lax.axis_size("fy")
    summed, msum, *edges = pl.pallas_call(
        functools.partial(local_kernel, nx, ny, halves),
        grid=(steps,),
        out_shape=[
            jax.ShapeDtypeStruct((halves, planes, rows, LANES), F32),
            jax.ShapeDtypeStruct((halves, rows, LANES), F32),
            edge_col, edge_col, edge_row, edge_row,
        ],
        in_specs=[half_spec(h) for h in range(halves)]
        + [whole((rows, cols))] * 2 + [whole((cols, cols))] * 2,
        out_specs=[
            pl.BlockSpec((halves, chunk, rows, LANES), lambda i: (0, i, 0, 0)),
            whole((halves, rows, LANES)), whole((rows, LANES)), whole((rows, LANES)),
            whole((row_slots, cols)), whole((row_slots, cols)),
        ],
        scratch_shapes=[
            pltpu.VMEM((halves, chunk, rows, LANES), F32),
            pltpu.VMEM((4, elements, cols), F32),
            pltpu.VMEM((4, elements, cols), F32),
            pltpu.VMEM((halves, 2, rows, LANES), F32),
            pltpu.VMEM((4, elements, LANES), F32),
            pltpu.VMEM((4, elements, LANES), F32),
            pltpu.VMEM((rows, LANES), F32),
            pltpu.VMEM((rows, LANES), F32),
            pltpu.VMEM((row_slots, cols), F32),
            pltpu.VMEM((row_slots, cols), F32),
            pltpu.VMEM((2, rows, LANES), F32),
            pltpu.VMEM((2, row_slots, cols), F32),
            pltpu.VMEM((4, TILE, LANES), F32),
            pltpu.SemaphoreType.DMA((8,)),
            pltpu.SemaphoreType.DMA((8,)),
        ],
        compiler_params=pltpu.CompilerParams(
            collective_id=0, has_side_effects=True, vmem_limit_bytes=VMEM_LIMIT
        ),
        name="local_terms",
    )(*[flat] * halves, jacobian, viscosity, khi, klo)

    vmem = pl.BlockSpec(memory_space=pltpu.VMEM)
    depth = -(-levels // 16) * 16
    parts = 4
    banded = (planes, rows // TILE, TILE, cols)
    anywhere = pl.BlockSpec(memory_space=pl.ANY)
    result = pl.pallas_call(
        column_kernel,
        out_shape=jax.ShapeDtypeStruct(banded, F32),
        in_specs=[pl.BlockSpec(memory_space=pltpu.SMEM), vmem] + [anywhere] * 7,
        out_specs=anywhere,
        scratch_shapes=[
            pltpu.VMEM(banded, F32),
            pltpu.VMEM((halves, planes, rows, LANES), F32),
            pltpu.VMEM(banded, F32),
            pltpu.VMEM((TILE, depth, cols), F32),
            pltpu.VMEM((TILE, depth, cols), F32),
            pltpu.VMEM((rows, cols), F32),
            pltpu.SemaphoreType.DMA((rows // TILE,)),
            pltpu.SemaphoreType.DMA((parts,)),
            pltpu.SemaphoreType.DMA((parts,)),
            pltpu.SemaphoreType.DMA((5,)),
            pltpu.VMEM((halves, rows, LANES), F32),
            pltpu.VMEM((rows, LANES), F32),
            pltpu.VMEM((rows, LANES), F32),
            pltpu.VMEM((row_slots, cols), F32),
            pltpu.VMEM((row_slots, cols), F32),
        ],
        compiler_params=pltpu.CompilerParams(vmem_limit_bytes=VMEM_LIMIT),
        name="column_step",
    )(convect_dest.reshape(rows), mixing, flat.reshape(banded), summed, msum, *edges)
    return result.reshape(air_state.shape)


def solution(mesh):
    placed = (P(None, None, "fy", "fx"), P("fy", "fx"), P("fy", "fx"), P(), P("fy", "fx"))
    return jax.shard_map(
        body, mesh=mesh, in_specs=placed, out_specs=P(None, None, "fy", "fx"), check_vma=False
    )
```
